32 devices in a mesh: row: 8 (over z, x), col: 4 (over y, core).
Axes of the slice: x: 2, y: 2, z: 4, core: 2. Of those that a mesh axis runs over, the one named last changes fastest.
Arguments:
- queries: bfloat16 [64, 64, 768], P('row', 'col'), may hold values from -6 to 6
- keys: bfloat16 [64, 64, 768], P('row', 'col'), may hold values from -6 to 6
- values: bfloat16 [64, 64, 768], P('row', 'col'), may hold values from -6 to 6
- d_out: bfloat16 [64, 64, 768], P('row', 'col'), may hold values from -6 to 6
- extents: int32 [2, 4, 4], replicated, may hold values from 4 to 16, as said below
- rel_bias: float32 [12, 13, 13], replicated, may hold values from -4 to 4
Outputs:
- attended: bfloat16 [64, 64, 768], P('row', 'col')
- d_queries: bfloat16 [64, 64, 768], P('row', 'col')
- d_keys: bfloat16 [64, 64, 768], P('row', 'col')
- d_values: bfloat16 [64, 64, 768], P('row', 'col')
- d_rel_bias: float32 [12, 13, 13], replicated
The draws below stay inside these ranges and needn't reach their ends.
Inputs may be any that keep to these rules, and one draw needn't show every extreme that they name: `extents`: every slot holds one image at its top-left corner.
All inputs are finite; a program needn't handle non-finite values.
Results may differ from the reference program's by a relative error of at most 0.011.
Values may be sent and summed in bfloat16 or wider, within the bound.
A program may use at most 64 MiB of HBM per device.

```python
import jax
import jax.numpy as jnp
from jax import lax

HEADS = 12
HDIM = 64
RAD = 6
GROUP = 4
TH = 8
TW = 16
WIDTH = 768
SPAN = 13
IH = 64
IW = 64
PANEL = 16
PR = 4
PC = 4
N_ROW = 8
N_COL = 4


def drawn_pair(key):
    base = jax.random.fold_in(key, 17)
    key_q, key_k = jax.random.split(base, 2)
    shape = (IH, IW, HEADS * HDIM)
    queries = jnp.clip(jax.random.normal(key_q, shape, jnp.float32), -6.0, 6.0)
    keys = jnp.clip(jax.random.normal(key_k, shape, jnp.float32), -6.0, 6.0)
    return (queries, keys)


def draw_queries(key, part):
    return drawn_pair(key)[0].astype(jnp.bfloat16)


def draw_keys(key, part):
    return drawn_pair(key)[1].astype(jnp.bfloat16)


def draw_extents(key, part):
    key_h, key_w = jax.random.split(jax.random.fold_in(key, 29))
    heights = jax.random.randint(key_h, (PR, PC), PANEL // 4, PANEL + 1)
    widths = jax.random.randint(key_w, (PR, PC), PANEL // 4, PANEL + 1)
    heights = heights.at[0, 0].set(PANEL).at[PR - 1, PC - 1].set(PANEL // 4)
    widths = widths.at[0, 0].set(PANEL).at[PR - 1, PC - 1].set(PANEL // 4)
    return jnp.stack([heights, widths]).astype(jnp.int32)


def block_levels(key, shape, cuts, smallest, largest):
    loudness = 1.0
    for position, parts in cuts:
        steps = jax.random.uniform(jax.random.fold_in(jax.random.fold_in(key, 6), position), (parts,), jnp.float32, smallest / len(cuts), largest / len(cuts))
        loudness = loudness * jnp.repeat(jnp.exp(steps), shape[position] // parts).reshape((-1,) + (1,) * (len(shape) - 1 - position))
    return loudness


def noise(key, dims, deviation, reach, shards=(), kind=jnp.bfloat16):
    level = block_levels(key, dims, shards, -0.22, 0.18) if shards else 1.0
    array = jax.random.normal(key, dims, jnp.float32) * deviation * level
    return jnp.minimum(jnp.maximum(array, -reach), reach).astype(kind)


def setup_inputs(seed: int = 0) -> dict:
    key_list = jax.random.split(jax.random.key(seed), 7)
    return {
        "queries": draw_queries(jax.random.fold_in(key_list[6], 71), 0),
        "keys": draw_keys(jax.random.fold_in(key_list[6], 71), 0),
        "values": noise(key_list[2], (IH, IW, WIDTH), 1.0, 6.0, ((0, 8), (1, 4))),
        "d_out": noise(key_list[3], (IH, IW, WIDTH), 1.0, 6.0, ((0, 8), (1, 4))),
        "extents": draw_extents(jax.random.fold_in(key_list[6], 71), 0),
        "rel_bias": noise(key_list[5], (HEADS, SPAN, SPAN), 1.0, 4.0, (), jnp.float32),
    }


HIGH = lax.Precision.HIGHEST


def offset_tables(group_rows, tile_cols, radius):
    span_size = 2 * radius + 1
    query_rows = jnp.arange(group_rows, dtype=jnp.int32)
    key_rows = jnp.arange(group_rows + 2 * radius, dtype=jnp.int32)
    row_offsets = ((key_rows[None, :] - query_rows[:, None])[:, :, None] == jnp.arange(span_size, dtype=jnp.int32)[None, None, :]).astype(jnp.float32)
    query_cols = jnp.arange(tile_cols, dtype=jnp.int32)
    key_cols = jnp.arange(tile_cols + 2 * radius, dtype=jnp.int32)
    col_offsets = ((key_cols[None, :] - query_cols[:, None])[:, :, None] == jnp.arange(span_size, dtype=jnp.int32)[None, None, :]).astype(jnp.float32)
    return row_offsets, col_offsets


def canvas_valid(extents):
    rows = jnp.arange(IH, dtype=jnp.int32)
    cols = jnp.arange(IW, dtype=jnp.int32)
    heights = extents[0][rows // PANEL][:, cols // PANEL]
    widths = extents[1][rows // PANEL][:, cols // PANEL]
    return ((rows % PANEL)[:, None] < heights) & ((cols % PANEL)[None, :] < widths)


def offset_sum(dscore, row_offsets, col_offsets):
    head_count = dscore.shape[0]
    group_rows, band_rows = row_offsets.shape[0], row_offsets.shape[1]
    tile_cols, band_cols = col_offsets.shape[0], col_offsets.shape[1]
    shaped = dscore.reshape(head_count, group_rows, tile_cols, band_rows, band_cols)
    by_col = jnp.einsum("hicjm,cmb->hijb", shaped, col_offsets, precision=HIGH)
    return jnp.einsum("hijb,ija->hab", by_col, row_offsets, precision=HIGH)


def tile_pass(query_tile, grad_tile, band, band_valid, bias, window, row_offsets, col_offsets):
    tile_rows, tile_cols, channels = query_tile.shape
    head_count = bias.shape[0]
    head_size = channels // head_count
    scale = head_size ** -0.5
    band_cols = band.shape[2]
    radius = (band_cols - tile_cols) // 2
    band_rows = GROUP + 2 * radius
    out_pieces = []
    dq_pieces = []
    grads = jnp.zeros((2, band.shape[1], band_cols, channels), jnp.float32)
    bias_grad = jnp.zeros((head_count, row_offsets.shape[2], col_offsets.shape[2]), jnp.float32)
    for block in range(tile_rows // GROUP):
        first = block * GROUP
        query_heads = query_tile[first:first + GROUP].reshape(GROUP * tile_cols, head_count, head_size).astype(jnp.float32)
        key_heads = band[0, first:first + band_rows].reshape(band_rows * band_cols, head_count, head_size).astype(jnp.float32)
        value_heads = band[1, first:first + band_rows].reshape(band_rows * band_cols, head_count, head_size).astype(jnp.float32)
        valid_query = band_valid[first + radius:first + radius + GROUP, radius:radius + tile_cols].reshape(-1)
        valid_key = band_valid[first:first + band_rows].reshape(-1)
        allowed = window & valid_query[:, None] & valid_key[None, :]
        score = jnp.einsum("qhd,khd->hqk", query_heads, key_heads, precision=HIGH) * scale + bias
        score = jnp.where(allowed[None], score, -1e30)
        highest = jnp.max(score, axis=-1, keepdims=True)
        weights = jnp.exp(score - highest)
        prob = weights / jnp.sum(weights, axis=-1, keepdims=True)
        prob_b = lax.optimization_barrier(prob.astype(jnp.bfloat16)).astype(jnp.float32)
        output = jnp.einsum("hqk,khd->qhd", prob_b, value_heads, precision=HIGH)
        out_pieces.append(jnp.where(valid_query[:, None, None], output, 0.0).astype(jnp.bfloat16).reshape(GROUP, tile_cols, channels))
        grad_rows = grad_tile[first:first + GROUP].reshape(GROUP * tile_cols, head_count, head_size).astype(jnp.float32)
        grad_heads = jnp.where(valid_query[:, None, None], grad_rows, 0.0)
        delta = jnp.sum(grad_heads * output, axis=-1)
        dprob = jnp.einsum("qhd,khd->hqk", grad_heads, value_heads, precision=HIGH)
        dscore = prob * (dprob - jnp.transpose(delta)[:, :, None])
        dscore_b = lax.optimization_barrier(dscore.astype(jnp.bfloat16)).astype(jnp.float32)
        dq_block = jnp.einsum("hqk,khd->qhd", dscore_b, key_heads, precision=HIGH) * scale
        dq_pieces.append(dq_block.astype(jnp.bfloat16).reshape(GROUP, tile_cols, channels))
        dk_block = jnp.einsum("hqk,qhd->khd", dscore_b, query_heads, precision=HIGH) * scale
        dv_block = jnp.einsum("hqk,qhd->khd", prob_b, grad_heads, precision=HIGH)
        grads = grads.at[:, first:first + band_rows].add(jnp.stack([dk_block, dv_block]).reshape(2, band_rows, band_cols, channels))
        bias_grad = bias_grad + offset_sum(dscore, row_offsets, col_offsets)
    return jnp.concatenate(out_pieces, 0), jnp.concatenate(dq_pieces, 0), grads, bias_grad


def reference(queries, keys, values, d_out, extents, rel_bias):
    channels = HEADS * HDIM
    band_rows = GROUP + 2 * RAD
    band_cols = TW + 2 * RAD
    row_offsets, col_offsets = offset_tables(GROUP, TW, RAD)
    bias = jnp.einsum("hab,ija,cmb->hicjm", rel_bias.astype(jnp.float32), row_offsets, col_offsets, precision=HIGH).reshape(HEADS, GROUP * TW, band_rows * band_cols)
    window = (jnp.sum(row_offsets, -1)[:, None, :, None] * jnp.sum(col_offsets, -1)[None, :, None, :] > 0.5).reshape(GROUP * TW, band_rows * band_cols)
    valid = jnp.pad(canvas_valid(extents), RAD)
    band_all = jnp.pad(jnp.stack([keys, values]), ((0, 0), (RAD, RAD), (RAD, RAD), (0, 0)))
    zero = jnp.zeros((), jnp.int32)

    def step(carry, index):
        accum, bias_total = carry
        row_start = ((index // N_COL) * TH).astype(jnp.int32)
        col_start = ((index % N_COL) * TW).astype(jnp.int32)
        query_tile = lax.dynamic_slice(queries, (row_start, col_start, zero), (TH, TW, channels))
        grad_tile = lax.dynamic_slice(d_out, (row_start, col_start, zero), (TH, TW, channels))
        band = lax.dynamic_slice(band_all, (zero, row_start, col_start, zero), (2, TH + 2 * RAD, band_cols, channels))
        band_valid = lax.dynamic_slice(valid, (row_start, col_start), (TH + 2 * RAD, band_cols))
        out_tile, dq_tile, grads, bias_part = tile_pass(query_tile, grad_tile, band, band_valid, bias, window, row_offsets, col_offsets)
        older = lax.dynamic_slice(accum, (zero, row_start, col_start, zero), grads.shape)
        accum = lax.dynamic_update_slice(accum, older + grads, (zero, row_start, col_start, zero))
        return (accum, bias_total + bias_part), (out_tile, dq_tile)

    start = (jnp.zeros((2, IH + 2 * RAD, IW + 2 * RAD, channels), jnp.float32), jnp.zeros((HEADS, 2 * RAD + 1, 2 * RAD + 1), jnp.float32))
    (accum, bias_total), (out_tiles, dq_tiles) = lax.scan(step, start, jnp.arange(N_ROW * N_COL, dtype=jnp.int32))

    def assemble(tiles):
        return jnp.transpose(tiles.reshape(N_ROW, N_COL, TH, TW, channels), (0, 2, 1, 3, 4)).reshape(IH, IW, channels)

    d_keys = accum[0, RAD:RAD + IH, RAD:RAD + IW].astype(jnp.bfloat16)
    d_values = accum[1, RAD:RAD + IH, RAD:RAD + IW].astype(jnp.bfloat16)
    return (assemble(out_tiles), assemble(dq_tiles), d_keys, d_values, bias_total)
```

```python
import functools

import jax
import jax.numpy as jnp
from jax import lax
from jax.experimental import pallas as pl
from jax.experimental.pallas import tpu as pltpu
from jax.sharding import PartitionSpec as P

MESH = pl.DeviceIdType.MESH
F32 = jnp.float32
BF16 = jnp.bfloat16
CHUNKS = 3
NEG = -1e30


def nt(a, b):
    return lax.dot_general(a, b, (((1,), (1,)), ((), ())), preferred_element_type=F32)


def nn(a, b):
    return lax.dot_general(a, b, (((1,), (0,)), ((), ())), preferred_element_type=F32)


def halves(x):
    high = x.astype(BF16)
    low = (x - high.astype(F32)).astype(BF16)
    return jnp.concatenate([high, low], axis=0)


def kernel(
    n_row, n_col, tr, tc, rad,
    q_ref, k_ref, v_ref, g_ref, ext_ref, rel_ref,
    o_ref, dq_ref, dk_ref, dv_ref, rb_ref,
    kv, pack, bias, mask, table, dtable, centre, strip_out, strip_in, rows_out, rows_in,
    part, slots_r, slots_c,
    kr_s, kr_r, kc_s, kc_r, gc_s, gc_r, gr_s, gr_r, br_s, br_r, bc_s, bc_r,
):
    row, col = lax.axis_index("row"), lax.axis_index("col")
    nk = tr + 2 * rad
    nq = tr * tc
    half = tc // 2
    mid, side = nk * tc, nk * half
    halo = rad * tc
    chunks, _, keys, wide = kv.shape
    per = wide // 128
    pairs = chunks * per
    panels_r, panels_c = ext_ref.shape[1], ext_ref.shape[2]
    panel = 2 * tr

    up, down = row > 0, row < n_row - 1
    left, right = col > 0, col < n_col - 1
    row_down, row_up = lax.rem(row + 1, n_row), lax.rem(row + n_row - 1, n_row)
    col_right, col_left = lax.rem(col + 1, n_col), lax.rem(col + n_col - 1, n_col)

    barrier = pltpu.get_barrier_semaphore()
    for step in range(1, n_row):
        pl.semaphore_signal(
            barrier, inc=1, device_id=(lax.rem(row + step, n_row), col), device_id_type=MESH
        )
    for step in range(1, n_col):
        pl.semaphore_signal(
            barrier, inc=1, device_id=(row, lax.rem(col + step, n_col)), device_id_type=MESH
        )

    for c in range(chunks):
        kv[c, 0, halo : halo + nq, :] = k_ref[:, c * wide : (c + 1) * wide]
        kv[c, 1, halo : halo + nq, :] = v_ref[:, c * wide : (c + 1) * wide]
    pl.semaphore_wait(barrier, n_row - 1 + n_col - 1)

    def remote(src, dst, send, recv, to):
        return pltpu.make_async_remote_copy(
            src_ref=src, dst_ref=dst, send_sem=send, recv_sem=recv, device_id=to, device_id_type=MESH
        )

    def key_rows(c):
        return (
            remote(kv.at[c, :, nq + halo - halo : nq + halo], kv.at[c, :, 0:halo],
                   kr_s.at[c, 0], kr_r.at[c, 0], (row_down, col)),
            remote(kv.at[c, :, halo : 2 * halo], kv.at[c, :, halo + nq : mid],
                   kr_s.at[c, 1], kr_r.at[c, 1], (row_up, col)),
        )

    def key_cols(c):
        return (
            remote(pack.at[c, :, 0:side], kv.at[c, :, mid : mid + side],
                   kc_s.at[c, 0], kc_r.at[c, 0], (row, col_right)),
            remote(pack.at[c, :, side : 2 * side], kv.at[c, :, mid + side : mid + 2 * side],
                   kc_s.at[c, 1], kc_r.at[c, 1], (row, col_left)),
        )

    def grad_cols(c):
        return (
            remote(strip_out.at[c, :, side : 2 * side], strip_in.at[c, :, side : 2 * side],
                   gc_s.at[c, 0], gc_r.at[c, 0], (row, col_right)),
            remote(strip_out.at[c, :, 0:side], strip_in.at[c, :, 0:side],
                   gc_s.at[c, 1], gc_r.at[c, 1], (row, col_left)),
        )

    def grad_rows(c):
        return (
            remote(rows_out.at[c, :, halo : 2 * halo], rows_in.at[c, :, halo : 2 * halo],
                   gr_s.at[c, 0], gr_r.at[c, 0], (row_down, col)),
            remote(rows_out.at[c, :, 0:halo], rows_in.at[c, :, 0:halo],
                   gr_s.at[c, 1], gr_r.at[c, 1], (row_up, col)),
        )

    def start(copies, after, before):
        pl.when(after)(lambda: copies[0].start())
        pl.when(before)(lambda: copies[1].start())

    def arrive(copies, after, before):
        pl.when(before)(lambda: copies[0].wait_recv())
        pl.when(after)(lambda: copies[1].wait_recv())

    def sent(copies, after, before):
        pl.when(after)(lambda: copies[0].wait_send())
        pl.when(before)(lambda: copies[1].wait_send())

    for c in range(chunks):
        start(key_rows(c), down, up)

    @pl.when(jnp.logical_not(up))
    def _():
        kv[:, :, 0:halo, :] = jnp.zeros((chunks, 2, halo, wide), BF16)
        rows_in[:, :, halo : 2 * halo, :] = jnp.zeros((chunks, 2, halo, wide), BF16)

    @pl.when(jnp.logical_not(down))
    def _():
        kv[:, :, halo + nq : mid, :] = jnp.zeros((chunks, 2, halo, wide), BF16)
        rows_in[:, :, 0:halo, :] = jnp.zeros((chunks, 2, halo, wide), BF16)

    @pl.when(jnp.logical_not(left))
    def _():
        kv[:, :, mid : mid + side, :] = jnp.zeros((chunks, 2, side, wide), BF16)
        strip_in[:, :, side : 2 * side, :] = jnp.zeros((chunks, 2, side, wide), BF16)

    @pl.when(jnp.logical_not(right))
    def _():
        kv[:, :, mid + side : mid + 2 * side, :] = jnp.zeros((chunks, 2, side, wide), BF16)
        strip_in[:, :, 0:side, :] = jnp.zeros((chunks, 2, side, wide), BF16)

    tiles_n = table.shape[0]
    span_lanes = tiles_n * 128
    heads_pad = rel_ref.shape[0]
    cols2 = 2 * tc

    def one_hot(kc):
        lane = lax.broadcasted_iota(jnp.int32, (1, span_lanes), 1)
        a = nk - 1 - lane // tc
        b = kc - (half - rad) - lane % tc
        target = jnp.where((a >= 0) & (a < 16) & (b >= 0) & (b < 16), a * 16 + b, -1)
        place = lax.broadcasted_iota(jnp.int32, (256, span_lanes), 0)
        return jnp.where(place == target, 1.0, 0.0).astype(BF16)

    rel2 = halves(rel_ref[...])

    def fill_table(kc, carry):
        both = nn(rel2, one_hot(kc))
        both = both[:heads_pad] + both[heads_pad:]
        for t in range(tiles_n):
            table[t, pl.ds(kc, heads_pad, stride=cols2), :] = both[:, t * 128 : (t + 1) * 128]
        return carry

    lax.fori_loop(0, cols2, fill_table, 0)

    sub = lax.broadcasted_iota(jnp.int32, (cols2, nq), 0)
    lane = lax.broadcasted_iota(jnp.int32, (cols2, nq), 1)
    q_row, q_col = lane // tc, lane % tc
    q_high = ext_ref[0, (row * tr) // panel, col]
    q_wide = ext_ref[1, (row * tr) // panel, col]
    q_first = lax.rem(row * tr, panel)
    col_diff = sub - (half - rad) - q_col
    fits = (
        (q_row + q_first < q_high) & (q_col < q_wide) & (col_diff >= 0) & (col_diff <= 2 * rad)
    )
    col_mod = lax.rem(sub + half, tc)
    for kr in range(nk):
        r = row * tr - rad + kr
        inside = (r >= 0) & (r < n_row * tr)
        pr = jnp.clip(r, 0, n_row * tr - 1) // panel
        widths = []
        for shift in (-1, 0, 1):
            pc = jnp.clip(col + shift, 0, panels_c - 1)
            there = inside & (col + shift >= 0) & (col + shift < n_col)
            there = there & (r - pr * panel < ext_ref[0, pr, pc])
            widths.append(jnp.where(there, ext_ref[1, pr, pc], 0))
        width = jnp.where(
            sub < half, widths[0], jnp.where(sub < half + tc, widths[1], widths[2])
        )
        row_diff = kr - q_row
        allowed = fits & (row_diff >= 0) & (row_diff <= 2 * rad) & (col_mod < width)
        mask[kr] = jnp.where(allowed, 0.0, NEG)

    def fill_bias(p, carry):
        for hh in range(2):
            base = pl.multiple_of((p * 2 + hh) * cols2, cols2)
            tiles = [table[t, pl.ds(base, cols2), :] for t in range(tiles_n)]
            lo = hh * 128
            for kr in range(nk):
                off = (nk - 1 - kr) * tc
                t, s = off // 128, off % 128
                x = tiles[t]
                if s:
                    x = pltpu.roll(jnp.where(lane >= s, x, tiles[t + 1]), 128 - s, 1)
                x = x + mask[kr]
                bias[p, mid + kr * half : mid + (kr + 1) * half, lo : lo + 128] = x[:half]
                bias[p, kr * tc : (kr + 1) * tc, lo : lo + 128] = x[half : half + tc]
                at = mid + side + kr * half
                bias[p, at : at + half, lo : lo + 128] = x[half + tc :]
        return carry

    lax.fori_loop(0, pairs, fill_bias, 0)

    q_sub = lax.broadcasted_iota(jnp.int32, (nq, 128), 0)
    ch = lax.broadcasted_iota(jnp.int32, (nq, 128), 1)
    q_valid = (q_sub // tc + q_first < q_high) & (q_sub % tc < q_wide)

    def send_cols(c):
        arrive(key_rows(c), down, up)
        for i in range(2):
            x = kv[c, i, 0:mid, :].astype(F32).reshape(nk, tc, wide)
            pack[c, i, 0:side, :] = x[:, half:].reshape(side, wide).astype(BF16)
            pack[c, i, side : 2 * side, :] = x[:, :half].reshape(side, wide).astype(BF16)
        start(key_cols(c), right, left)

    def block(x):
        zero = jnp.zeros_like(x)
        return jnp.concatenate(
            [jnp.where(ch < 64, x, zero), jnp.where(ch < 64, zero, x)], axis=0
        ).astype(BF16)

    def compute(c, pp):
        p = c * per + pp
        at = pl.multiple_of(pp * 128, 128)
        full = pl.multiple_of(p * 128, 128)
        k2 = kv[c, 0, :, pl.ds(at, 128)]
        v2 = kv[c, 1, :, pl.ds(at, 128)]
        qb = block(q_ref[:, pl.ds(full, 128)].astype(F32) * 0.125)
        gb = block(jnp.where(q_valid, g_ref[:, pl.ds(full, 128)].astype(F32), 0.0))
        score = nt(k2, qb) + bias[p]
        weights = jnp.exp(score - jnp.max(score, axis=0, keepdims=True))
        prob = weights * (1.0 / jnp.sum(weights, axis=0, keepdims=True))
        prob_b = prob.astype(BF16)
        dprob = nt(v2, gb)
        delta = jnp.sum(prob_b.astype(F32) * dprob, axis=0, keepdims=True)
        ds = prob * (dprob - delta)
        ds_b = ds.astype(BF16)

        def back(x, scores):
            both = nn(x.T, scores)
            return jnp.concatenate([both[:64, :128], both[64:, 128:]], axis=0).T

        o_ref[:, pl.ds(full, 128)] = jnp.where(q_valid, back(v2, prob_b), 0.0).astype(BF16)
        dq_ref[:, pl.ds(full, 128)] = (back(k2, ds_b) * 0.125).astype(BF16)
        for i, grad in enumerate((nn(ds_b, qb), nn(prob_b, gb))):
            centre[c, i, :, pl.ds(at, 128)] = grad[:mid]
            strip_out[c, i, :, pl.ds(at, 128)] = grad[mid:].astype(BF16)
        for hh in range(2):
            d = ds[:, hh * 128 : (hh + 1) * 128]
            sums = [jnp.zeros((cols2, nq), F32) for _ in range(tiles_n)]
            for kr in range(nk):
                off = (nk - 1 - kr) * tc
                t, s = off // 128, off % 128
                at2 = mid + kr * half
                x = jnp.concatenate(
                    [d[at2 : at2 + half], d[kr * tc : (kr + 1) * tc],
                     d[side + at2 : side + at2 + half]], axis=0,
                )
                if s:
                    x = pltpu.roll(x, s, 1)
                    sums[t] = sums[t] + jnp.where(lane >= s, x, 0.0)
                    sums[t + 1] = sums[t + 1] + jnp.where(lane >= s, 0.0, x)
                else:
                    sums[t] = sums[t] + x
            base = pl.multiple_of((p * 2 + hh) * cols2, cols2)
            for t, total in enumerate(sums):
                dtable[t, pl.ds(base, cols2), :] = total

    def send_rows(c):
        arrive(grad_cols(c), right, left)
        for i in range(2):
            x = centre[c, i].reshape(nk, tc, wide)
            y = jnp.concatenate(
                [strip_in[c, i, side : 2 * side, :].astype(F32).reshape(nk, half, wide),
                 strip_in[c, i, 0:side, :].astype(F32).reshape(nk, half, wide)], axis=1,
            )
            total = (x + y).reshape(mid, wide)
            rows_out[c, i, 0:halo, :] = total[:halo].astype(BF16)
            rows_out[c, i, halo : 2 * halo, :] = total[halo + nq :].astype(BF16)
            centre[c, i, halo : halo + nq, :] = total[halo : halo + nq]
        start(grad_rows(c), down, up)

    send_cols(0)
    for c in range(chunks):
        if c + 1 < chunks:
            send_cols(c + 1)
        arrive(key_cols(c), right, left)

        def one(pp, carry, c=c):
            compute(c, pp)
            return carry

        lax.fori_loop(0, per, one, 0)
        start(grad_cols(c), right, left)
        if c:
            send_rows(c - 1)
    unused = heads_pad - pairs * 2
    dtable[:, pairs * 2 * cols2 :, :] = jnp.zeros((tiles_n, unused * cols2, 128), F32)

    def gather_bias(kc, total):
        x = jnp.concatenate(
            [dtable[t, pl.ds(kc, heads_pad, stride=cols2), :] for t in range(tiles_n)], axis=1
        )
        both = nt(halves(x), one_hot(kc))
        return total + both[:heads_pad] + both[heads_pad:]

    part[...] = lax.fori_loop(0, cols2, gather_bias, jnp.zeros((heads_pad, 256), F32))

    def spread(slots, me, count, send, recv, to):
        copies = [
            remote(part, slots.at[me], send.at[k], recv.at[k], to(lax.rem(me + k, count)))
            for k in range(1, count)
        ]
        return copies

    over_rows = spread(slots_r, row, n_row, br_s, br_r, lambda r: (r, col))
    for copy in over_rows:
        copy.start()
    slots_r[row] = part[...]
    send_rows(chunks - 1)
    for copy in over_rows:
        copy.wait()
    total = slots_r[0]
    for k in range(1, n_row):
        total = total + slots_r[k]
    part[...] = total
    over_cols = spread(slots_c, col, n_col, bc_s, bc_r, lambda k: (row, k))
    for copy in over_cols:
        copy.start()
    slots_c[col] = part[...]

    for c in range(chunks):
        arrive(grad_rows(c), down, up)
        for i, out in enumerate((dk_ref, dv_ref)):
            x = centre[c, i, halo : halo + nq, :]
            fill = jnp.zeros((nq - halo, wide), F32)
            x = x + jnp.concatenate([rows_in[c, i, halo : 2 * halo, :].astype(F32), fill], axis=0)
            x = x + jnp.concatenate([fill, rows_in[c, i, 0:halo, :].astype(F32)], axis=0)
            out[:, c * wide : (c + 1) * wide] = x.astype(BF16)
    for copy in over_cols:
        copy.wait()
    total = slots_c[0]
    for k in range(1, n_col):
        total = total + slots_c[k]
    rb_ref[...] = total
    for c in range(chunks):
        sent(key_rows(c), down, up)
        sent(key_cols(c), right, left)
        sent(grad_cols(c), right, left)
        sent(grad_rows(c), down, up)


def shards(n_row, n_col, queries, keys, values, d_out, extents, rel_bias):
    tr, tc, channels = queries.shape
    heads, span = rel_bias.shape[0], rel_bias.shape[1]
    rad = (span - 1) // 2
    nq, nk = tr * tc, tr + 2 * rad
    wide = channels // CHUNKS
    mid, side, halo = nk * tc, nk * (tc // 2), rad * tc
    lanes = -(-((nk + tr - 1) * tc) // 128) * 128
    flat = [x.reshape(nq, channels) for x in (queries, keys, values, d_out)]
    rel = jnp.pad(rel_bias, ((0, 16 - heads), (0, 16 - span), (0, 16 - span))).reshape(16, 256)
    vmem = pl.BlockSpec(memory_space=pltpu.VMEM)
    dma = pltpu.SemaphoreType.DMA
    out = jax.ShapeDtypeStruct((nq, channels), BF16)
    *big, d_rel = pl.pallas_call(
        functools.partial(kernel, n_row, n_col, tr, tc, rad),
        out_shape=[out, out, out, out, jax.ShapeDtypeStruct((16, 256), F32)],
        in_specs=[vmem] * 4 + [pl.BlockSpec(memory_space=pltpu.SMEM), vmem],
        out_specs=[vmem] * 5,
        scratch_shapes=[
            pltpu.VMEM((CHUNKS, 2, mid + 2 * side, wide), BF16),
            pltpu.VMEM((CHUNKS, 2, 2 * side, wide), BF16),
            pltpu.VMEM((channels // 128, mid + 2 * side, 256), F32),
            pltpu.VMEM((nk, 2 * tc, nq), F32),
            pltpu.VMEM((lanes // 128, 16 * 2 * tc, 128), F32),
            pltpu.VMEM((lanes // 128, 16 * 2 * tc, 128), F32),
            pltpu.VMEM((CHUNKS, 2, mid, wide), F32),
            pltpu.VMEM((CHUNKS, 2, 2 * side, wide), BF16),
            pltpu.VMEM((CHUNKS, 2, 2 * side, wide), BF16),
            pltpu.VMEM((CHUNKS, 2, 2 * halo, wide), BF16),
            pltpu.VMEM((CHUNKS, 2, 2 * halo, wide), BF16),
            pltpu.VMEM((16, 256), F32),
            pltpu.VMEM((n_row, 16, 256), F32),
            pltpu.VMEM((n_col, 16, 256), F32),
        ]
        + [dma((CHUNKS, 2))] * 8
        + [dma((n_row,)), dma((n_row,)), dma((n_col,)), dma((n_col,))],
        compiler_params=pltpu.CompilerParams(
            collective_id=0, has_side_effects=True, vmem_limit_bytes=48 * 1024 * 1024
        ),
        cost_estimate=pl.CostEstimate(
            flops=12 * 12 * 128 * 640 * 64, bytes_accessed=8 * 200000, transcendentals=12 * 128 * 640
        ),
    )(*flat, extents, rel)
    big = [x.reshape(tr, tc, channels) for x in big]
    return (*big, d_rel.reshape(16, 16, 16)[:heads, :span, :span])


def solution(mesh):
    tile = P("row", "col", None)
    return jax.shard_map(
        functools.partial(shards, mesh.shape["row"], mesh.shape["col"]),
        mesh=mesh,
        in_specs=(tile, tile, tile, tile, P(), P()),
        out_specs=(tile, tile, tile, tile, P()),
        check_vma=False,
    )
```

```python
import functools

import jax
import jax.numpy as jnp
from jax import lax
from jax.experimental import pallas as pl
from jax.experimental.pallas import tpu as pltpu
from jax.sharding import PartitionSpec as P

MESH = pl.DeviceIdType.MESH
F32 = jnp.float32
BF16 = jnp.bfloat16
CHUNKS = 6
NEG = -1e30


def nt(a, b):
    return lax.dot_general(a, b, (((1,), (1,)), ((), ())), preferred_element_type=F32)


def nn(a, b):
    return lax.dot_general(a, b, (((1,), (0,)), ((), ())), preferred_element_type=F32)


def halves(x):
    high = x.astype(BF16)
    low = (x - high.astype(F32)).astype(BF16)
    return jnp.concatenate([high, low], axis=0)


def kernel(
    n_row, n_col, tr, tc, rad,
    q_hbm, k_hbm, v_hbm, g_hbm, ext_ref, rel_ref,
    o_ref, dq_ref, dk_ref, dv_ref, rb_ref,
    q_ref, g_ref, kv, pack, bias, mask, rel_pad, turned, table, dtable, centre, strip_out, strip_in, rows_out, rows_in,
    part, slots_r, slots_c,
    in_sem, kr_s, kr_r, kc_s, kc_r, gc_s, gc_r, gr_s, gr_r, br_s, br_r, bc_s, bc_r,
):
    row, col = lax.axis_index("row"), lax.axis_index("col")
    nk = tr + 2 * rad
    nq = tr * tc
    half = tc // 2
    mid, side = nk * tc, nk * half
    halo = rad * tc
    chunks, _, keys, wide = kv.shape
    per = wide // 128
    pairs = chunks * per
    panels_c = ext_ref.shape[2]
    panel = 2 * tr

    up, down = row > 0, row < n_row - 1
    left, right = col > 0, col < n_col - 1
    row_down, row_up = lax.rem(row + 1, n_row), lax.rem(row + n_row - 1, n_row)
    col_right, col_left = lax.rem(col + 1, n_col), lax.rem(col + n_col - 1, n_col)

    loads = [
        pltpu.make_async_copy(
            source.at[:, c * wide : (c + 1) * wide],
            kv.at[c, i, halo : halo + nq],
            in_sem.at[2 * c + i],
        )
        for c in range(chunks)
        for i, source in enumerate((k_hbm, v_hbm))
    ]
    late = [
        pltpu.make_async_copy(q_hbm, q_ref, in_sem.at[2 * chunks]),
        pltpu.make_async_copy(g_hbm, g_ref, in_sem.at[2 * chunks + 1]),
    ]
    for copy in loads + late:
        copy.start()
    barrier = pltpu.get_barrier_semaphore()
    for step in range(1, n_row):
        pl.semaphore_signal(
            barrier, inc=1, device_id=(lax.rem(row + step, n_row), col), device_id_type=MESH
        )
    for step in range(1, n_col):
        pl.semaphore_signal(
            barrier, inc=1, device_id=(row, lax.rem(col + step, n_col)), device_id_type=MESH
        )

    for copy in loads:
        copy.wait()
    pl.semaphore_wait(barrier, n_row - 1 + n_col - 1)

    def remote(src, dst, send, recv, to):
        return pltpu.make_async_remote_copy(
            src_ref=src, dst_ref=dst, send_sem=send, recv_sem=recv, device_id=to, device_id_type=MESH
        )

    def key_rows(c):
        return (
            remote(kv.at[c, :, nq + halo - halo : nq + halo], kv.at[c, :, 0:halo],
                   kr_s.at[c, 0], kr_r.at[c, 0], (row_down, col)),
            remote(kv.at[c, :, halo : 2 * halo], kv.at[c, :, halo + nq : mid],
                   kr_s.at[c, 1], kr_r.at[c, 1], (row_up, col)),
        )

    def key_cols(c):
        return (
            remote(pack.at[c, :, 0:side], kv.at[c, :, mid : mid + side],
                   kc_s.at[c, 0], kc_r.at[c, 0], (row, col_right)),
            remote(pack.at[c, :, side : 2 * side], kv.at[c, :, mid + side : mid + 2 * side],
                   kc_s.at[c, 1], kc_r.at[c, 1], (row, col_left)),
        )

    def grad_cols(c):
        return (
            remote(strip_out.at[c, :, side : 2 * side], strip_in.at[c, :, side : 2 * side],
                   gc_s.at[c, 0], gc_r.at[c, 0], (row, col_right)),
            remote(strip_out.at[c, :, 0:side], strip_in.at[c, :, 0:side],
                   gc_s.at[c, 1], gc_r.at[c, 1], (row, col_left)),
        )

    def grad_rows(c):
        return (
            remote(rows_out.at[c, :, halo : 2 * halo], rows_in.at[c, :, halo : 2 * halo],
                   gr_s.at[c, 0], gr_r.at[c, 0], (row_down, col)),
            remote(rows_out.at[c, :, 0:halo], rows_in.at[c, :, 0:halo],
                   gr_s.at[c, 1], gr_r.at[c, 1], (row_up, col)),
        )

    def start(copies, after, before):
        pl.when(after)(lambda: copies[0].start())
        pl.when(before)(lambda: copies[1].start())

    def arrive(copies, after, before):
        pl.when(before)(lambda: copies[0].wait_recv())
        pl.when(after)(lambda: copies[1].wait_recv())

    def sent(copies, after, before):
        pl.when(after)(lambda: copies[0].wait_send())
        pl.when(before)(lambda: copies[1].wait_send())

    for c in range(chunks):
        start(key_rows(c), down, up)

    @pl.when(jnp.logical_not(up))
    def _():
        kv[:, :, 0:halo, :] = jnp.zeros((chunks, 2, halo, wide), BF16)
        rows_in[:, :, halo : 2 * halo, :] = jnp.zeros((chunks, 2, halo, wide), BF16)

    @pl.when(jnp.logical_not(down))
    def _():
        kv[:, :, halo + nq : mid, :] = jnp.zeros((chunks, 2, halo, wide), BF16)
        rows_in[:, :, 0:halo, :] = jnp.zeros((chunks, 2, halo, wide), BF16)

    @pl.when(jnp.logical_not(left))
    def _():
        kv[:, :, mid : mid + side, :] = jnp.zeros((chunks, 2, side, wide), BF16)
        strip_in[:, :, side : 2 * side, :] = jnp.zeros((chunks, 2, side, wide), BF16)

    @pl.when(jnp.logical_not(right))
    def _():
        kv[:, :, mid + side : mid + 2 * side, :] = jnp.zeros((chunks, 2, side, wide), BF16)
        strip_in[:, :, 0:side, :] = jnp.zeros((chunks, 2, side, wide), BF16)

    tiles_n = table.shape[0]
    cols2 = 2 * tc
    fit = 128 // cols2
    groups = pairs * 2 // fit
    span = 2 * rad + 1
    edge = half - rad
    rel_pad[...] = jnp.zeros_like(rel_pad)

    def fill_rel(a, carry):
        for h in range(pairs * 2):
            at = (h % fit) * cols2
            rel_pad[h // fit, pl.ds(nk - 1 - a, 1), at : at + span] = rel_ref[h, pl.ds(a, 1), :]
        return carry

    lax.fori_loop(0, span, fill_rel, 0)
    steps = tiles_n * 128 // tc
    for g in range(groups):
        x = rel_pad[g]
        for qc in range(tc):
            turned[g, pl.ds(qc, steps, stride=tc), :] = pltpu.roll(x, qc + edge, 1)
        for t in range(tiles_n):
            table[t, g * 128 : (g + 1) * 128, :] = turned[g, t * 128 : (t + 1) * 128, :].T

    sub = lax.broadcasted_iota(jnp.int32, (cols2, nq), 0)
    lane = lax.broadcasted_iota(jnp.int32, (cols2, nq), 1)
    q_row, q_col = lane // tc, lane % tc
    q_high = ext_ref[0, (row * tr) // panel, col]
    q_wide = ext_ref[1, (row * tr) // panel, col]
    q_first = lax.rem(row * tr, panel)
    col_diff = sub - (half - rad) - q_col
    fits = (
        (q_row + q_first < q_high) & (q_col < q_wide) & (col_diff >= 0) & (col_diff <= 2 * rad)
    )
    col_mod = lax.rem(sub + half, tc)
    for kr in range(nk):
        r = row * tr - rad + kr
        inside = (r >= 0) & (r < n_row * tr)
        pr = jnp.clip(r, 0, n_row * tr - 1) // panel
        widths = []
        for shift in (-1, 0, 1):
            pc = jnp.clip(col + shift, 0, panels_c - 1)
            there = inside & (col + shift >= 0) & (col + shift < n_col)
            there = there & (r - pr * panel < ext_ref[0, pr, pc])
            widths.append(jnp.where(there, ext_ref[1, pr, pc], 0))
        width = jnp.where(
            sub < half, widths[0], jnp.where(sub < half + tc, widths[1], widths[2])
        )
        row_diff = kr - q_row
        allowed = fits & (row_diff >= 0) & (row_diff <= 2 * rad) & (col_mod < width)
        mask[kr] = jnp.where(allowed, 0.0, NEG)

    def fill_bias(p, carry):
        for hh in range(2):
            base = pl.multiple_of((p * 2 + hh) * cols2, cols2)
            tiles = [table[t, pl.ds(base, cols2), :] for t in range(tiles_n)]
            lo = hh * 128
            for kr in range(nk):
                off = (nk - 1 - kr) * tc
                t, s = off // 128, off % 128
                x = tiles[t]
                if s:
                    x = pltpu.roll(jnp.where(lane >= s, x, tiles[t + 1]), 128 - s, 1)
                x = x + mask[kr]
                bias[p, mid + kr * half : mid + (kr + 1) * half, lo : lo + 128] = x[:half]
                bias[p, kr * tc : (kr + 1) * tc, lo : lo + 128] = x[half : half + tc]
                at = mid + side + kr * half
                bias[p, at : at + half, lo : lo + 128] = x[half + tc :]
        return carry

    lax.fori_loop(0, pairs, fill_bias, 0)

    q_sub = lax.broadcasted_iota(jnp.int32, (nq, 128), 0)
    ch = lax.broadcasted_iota(jnp.int32, (nq, 128), 1)
    q_valid = (q_sub // tc + q_first < q_high) & (q_sub % tc < q_wide)

    def send_cols(c):
        arrive(key_rows(c), down, up)
        for i in range(2):
            x = kv[c, i, 0:mid, :].astype(F32).reshape(nk, tc, wide)
            pack[c, i, 0:side, :] = x[:, half:].reshape(side, wide).astype(BF16)
            pack[c, i, side : 2 * side, :] = x[:, :half].reshape(side, wide).astype(BF16)
        start(key_cols(c), right, left)

    def block(x):
        zero = jnp.zeros_like(x)
        return jnp.concatenate(
            [jnp.where(ch < 64, x, zero), jnp.where(ch < 64, zero, x)], axis=0
        ).astype(BF16)

    def compute(c, pp):
        p = c * per + pp
        at = pp * 128
        full = p * 128
        k2 = kv[c, 0, :, pl.ds(at, 128)]
        v2 = kv[c, 1, :, pl.ds(at, 128)]
        qb = block(q_ref[:, pl.ds(full, 128)].astype(F32) * 0.125)
        gb = block(jnp.where(q_valid, g_ref[:, pl.ds(full, 128)].astype(F32), 0.0))
        score = nt(k2, qb) + bias[p]
        weights = jnp.exp(score - jnp.max(score, axis=0, keepdims=True))
        prob = weights * (1.0 / jnp.sum(weights, axis=0, keepdims=True))
        prob_b = prob.astype(BF16)
        dprob = nt(v2, gb)
        delta = jnp.sum(prob_b.astype(F32) * dprob, axis=0, keepdims=True)
        ds = prob * (dprob - delta)
        ds_b = ds.astype(BF16)

        def back(x, scores):
            both = nn(x.T, scores)
            return jnp.concatenate([both[:64, :128], both[64:, 128:]], axis=0).T

        o_ref[:, pl.ds(full, 128)] = jnp.where(q_valid, back(v2, prob_b), 0.0).astype(BF16)
        dq_ref[:, pl.ds(full, 128)] = (back(k2, ds_b) * 0.125).astype(BF16)
        for i, grad in enumerate((nn(ds_b, qb), nn(prob_b, gb))):
            centre[c, i, :, pl.ds(at, 128)] = grad[:mid]
            strip_out[c, i, :, pl.ds(at, 128)] = grad[mid:].astype(BF16)
        for hh in range(2):
            d = ds[:, hh * 128 : (hh + 1) * 128]
            sums = [jnp.zeros((cols2, nq), F32) for _ in range(tiles_n)]
            for kr in range(nk):
                off = (nk - 1 - kr) * tc
                t, s = off // 128, off % 128
                at2 = mid + kr * half
                x = jnp.concatenate(
                    [d[at2 : at2 + half], d[kr * tc : (kr + 1) * tc],
                     d[side + at2 : side + at2 + half]], axis=0,
                )
                if s:
                    x = pltpu.roll(x, s, 1)
                    sums[t] = sums[t] + jnp.where(lane >= s, x, 0.0)
                    sums[t + 1] = sums[t + 1] + jnp.where(lane >= s, 0.0, x)
                else:
                    sums[t] = sums[t] + x
            base = pl.multiple_of((p * 2 + hh) * cols2, cols2)
            for t, total in enumerate(sums):
                dtable[t, pl.ds(base, cols2), :] = total

    def send_rows(c):
        arrive(grad_cols(c), right, left)
        for i in range(2):
            x = centre[c, i].reshape(nk, tc, wide)
            y = jnp.concatenate(
                [strip_in[c, i, side : 2 * side, :].astype(F32).reshape(nk, half, wide),
                 strip_in[c, i, 0:side, :].astype(F32).reshape(nk, half, wide)], axis=1,
            )
            total = (x + y).reshape(mid, wide)
            rows_out[c, i, 0:halo, :] = total[:halo].astype(BF16)
            rows_out[c, i, halo : 2 * halo, :] = total[halo + nq :].astype(BF16)
            centre[c, i, halo : halo + nq, :] = total[halo : halo + nq]
        start(grad_rows(c), down, up)

    for copy in late:
        copy.wait()
    send_cols(0)
    for c in range(chunks):
        if c + 1 < chunks:
            send_cols(c + 1)
        arrive(key_cols(c), right, left)

        for pp in range(per):
            compute(c, pp)
        start(grad_cols(c), right, left)
        if c:
            send_rows(c - 1)
    for g in range(groups):
        for t in range(tiles_n):
            turned[g, t * 128 : (t + 1) * 128, :] = dtable[t, g * 128 : (g + 1) * 128, :].T
        total = jnp.zeros((16, 128), F32)
        for qc in range(tc):
            x = turned[g, pl.ds((tr - 1) * tc + qc, 16, stride=tc), :]
            total = total + pltpu.roll(x, 128 - qc - edge, 1)
        part[g * 16 : (g + 1) * 16, :] = total

    def spread(slots, me, count, send, recv, to):
        copies = [
            remote(part, slots.at[me], send.at[k], recv.at[k], to(lax.rem(me + k, count)))
            for k in range(1, count)
        ]
        return copies

    over_rows = spread(slots_r, row, n_row, br_s, br_r, lambda r: (r, col))
    for copy in over_rows:
        copy.start()
    slots_r[row] = part[...]
    send_rows(chunks - 1)
    for copy in over_rows:
        copy.wait()
    total = slots_r[0]
    for k in range(1, n_row):
        total = total + slots_r[k]
    part[...] = total
    over_cols = spread(slots_c, col, n_col, bc_s, bc_r, lambda k: (row, k))
    for copy in over_cols:
        copy.start()
    slots_c[col] = part[...]

    for c in range(chunks):
        arrive(grad_rows(c), down, up)
        for i, out in enumerate((dk_ref, dv_ref)):
            x = centre[c, i, halo : halo + nq, :]
            fill = jnp.zeros((nq - halo, wide), F32)
            x = x + jnp.concatenate([rows_in[c, i, halo : 2 * halo, :].astype(F32), fill], axis=0)
            x = x + jnp.concatenate([fill, rows_in[c, i, 0:halo, :].astype(F32)], axis=0)
            out[:, c * wide : (c + 1) * wide] = x.astype(BF16)
    for copy in over_cols:
        copy.wait()
    total = slots_c[0]
    for k in range(1, n_col):
        total = total + slots_c[k]
    part[...] = total

    def give_rel(a, carry):
        for h in range(pairs * 2):
            at = (h % fit) * cols2
            row_at = h // fit * 16 + 2 * rad - a
            rb_ref[h, pl.ds(a, 1), :] = part[pl.ds(row_at, 1), at : at + span]
        return carry

    lax.fori_loop(0, span, give_rel, 0)
    for c in range(chunks):
        sent(key_rows(c), down, up)
        sent(key_cols(c), right, left)
        sent(grad_cols(c), right, left)
        sent(grad_rows(c), down, up)


def hand_over(*refs):
    sems = refs[-1]
    copies = [
        pltpu.make_async_copy(refs[i], refs[4 + i], sems.at[i]) for i in range(4)
    ]
    for copy in copies:
        copy.start()
    for copy in copies:
        copy.wait()


def shards(n_row, n_col, queries, keys, values, d_out, extents, rel_bias):
    tr, tc, channels = queries.shape
    heads, span = rel_bias.shape[0], rel_bias.shape[1]
    rad = (span - 1) // 2
    nq, nk = tr * tc, tr + 2 * rad
    wide = channels // CHUNKS
    mid, side, halo = nk * tc, nk * (tc // 2), rad * tc
    groups = heads * 2 * tc // 128
    lanes = -(-((nk + tr - 1) * tc) // 128) * 128
    flat = [x.reshape(nq, channels) for x in (queries, keys, values, d_out)]
    vmem = pl.BlockSpec(memory_space=pltpu.VMEM)
    hbm = pl.BlockSpec(memory_space=pltpu.HBM)
    dma = pltpu.SemaphoreType.DMA
    out = jax.ShapeDtypeStruct((nq, channels), BF16)
    *big, d_rel = pl.pallas_call(
        functools.partial(kernel, n_row, n_col, tr, tc, rad),
        out_shape=[out, out, out, out, jax.ShapeDtypeStruct(rel_bias.shape, F32)],
        in_specs=[hbm] * 4 + [pl.BlockSpec(memory_space=pltpu.SMEM), vmem],
        out_specs=[vmem] * 5,
        scratch_shapes=[
            pltpu.VMEM((nq, channels), BF16),
            pltpu.VMEM((nq, channels), BF16),
            pltpu.VMEM((CHUNKS, 2, mid + 2 * side, wide), BF16),
            pltpu.VMEM((CHUNKS, 2, 2 * side, wide), BF16),
            pltpu.VMEM((channels // 128, mid + 2 * side, 256), F32),
            pltpu.VMEM((nk, 2 * tc, nq), F32),
            pltpu.VMEM((groups, lanes // tc, 128), F32),
            pltpu.VMEM((groups, lanes, 128), F32),
            pltpu.VMEM((lanes // 128, heads * 2 * tc, 128), F32),
            pltpu.VMEM((lanes // 128, heads * 2 * tc, 128), F32),
            pltpu.VMEM((CHUNKS, 2, mid, wide), F32),
            pltpu.VMEM((CHUNKS, 2, 2 * side, wide), BF16),
            pltpu.VMEM((CHUNKS, 2, 2 * side, wide), BF16),
            pltpu.VMEM((CHUNKS, 2, 2 * halo, wide), BF16),
            pltpu.VMEM((CHUNKS, 2, 2 * halo, wide), BF16),
            pltpu.VMEM((groups * 16, 128), F32),
            pltpu.VMEM((n_row, groups * 16, 128), F32),
            pltpu.VMEM((n_col, groups * 16, 128), F32),
        ]
        + [dma((2 * CHUNKS + 2,))]
        + [dma((CHUNKS, 2))] * 8
        + [dma((n_row,)), dma((n_row,)), dma((n_col,)), dma((n_col,))],
        compiler_params=pltpu.CompilerParams(
            collective_id=0, has_side_effects=True, vmem_limit_bytes=63 * 1024 * 1024
        ),
        cost_estimate=pl.CostEstimate(
            flops=12 * 12 * 128 * 640 * 64, bytes_accessed=8 * 200000, transcendentals=12 * 128 * 640
        ),
    )(*flat, extents, rel_bias)
    anywhere = pl.BlockSpec(memory_space=pl.ANY)
    big = pl.pallas_call(
        hand_over,
        out_shape=[out] * 4,
        in_specs=[anywhere] * 4,
        out_specs=[hbm] * 4,
        scratch_shapes=[dma((4,))],
    )(*big)
    return (*(x.reshape(tr, tc, channels) for x in big), d_rel)


def solution(mesh):
    tile = P("row", "col", None)
    return jax.shard_map(
        functools.partial(shards, mesh.shape["row"], mesh.shape["col"]),
        mesh=mesh,
        in_specs=(tile, tile, tile, tile, P(), P()),
        out_specs=(tile, tile, tile, tile, P()),
        check_vma=False,
    )
```

```python
import functools

import jax
import jax.numpy as jnp
from jax import lax
from jax.experimental import pallas as pl
from jax.experimental.pallas import tpu as pltpu
from jax.sharding import PartitionSpec as P

MESH = pl.DeviceIdType.MESH
F32 = jnp.float32
BF16 = jnp.bfloat16
CHUNKS = 6
NEG = -1e30


def nt(a, b):
    return lax.dot_general(a, b, (((1,), (1,)), ((), ())), preferred_element_type=F32)


def nn(a, b):
    return lax.dot_general(a, b, (((1,), (0,)), ((), ())), preferred_element_type=F32)


def halves(x):
    high = x.astype(BF16)
    low = (x - high.astype(F32)).astype(BF16)
    return jnp.concatenate([high, low], axis=0)


def kernel(
    n_row, n_col, tr, tc, rad,
    q_hbm, k_hbm, v_hbm, g_hbm, ext_ref, rel_ref,
    o_ref, dq_ref, dk_ref, dv_ref, rb_ref,
    q_ref, g_ref, kv, pack, bias, mask, rel_pad, turned, table, dtable, centre, strip_out, strip_in, rows_out, rows_in,
    part, slots_r, slots_c,
    in_sem, kr_s, kr_r, kc_s, kc_r, gc_s, gc_r, gr_s, gr_r, br_s, br_r, bc_s, bc_r,
):
    row, col = lax.axis_index("row"), lax.axis_index("col")
    nk = tr + 2 * rad
    nq = tr * tc
    half = tc // 2
    mid, side = nk * tc, nk * half
    halo = rad * tc
    chunks, _, keys, wide = kv.shape
    per = wide // 128
    pairs = chunks * per
    panels_c = ext_ref.shape[2]
    panel = 2 * tr

    up, down = row > 0, row < n_row - 1
    left, right = col > 0, col < n_col - 1
    row_down, row_up = lax.rem(row + 1, n_row), lax.rem(row + n_row - 1, n_row)
    col_right, col_left = lax.rem(col + 1, n_col), lax.rem(col + n_col - 1, n_col)

    loads = [
        pltpu.make_async_copy(
            source.at[:, c * wide : (c + 1) * wide],
            kv.at[c, i, halo : halo + nq],
            in_sem.at[2 * c + i],
        )
        for c in range(chunks)
        for i, source in enumerate((k_hbm, v_hbm))
    ]
    late = [
        pltpu.make_async_copy(q_hbm, q_ref, in_sem.at[2 * chunks]),
        pltpu.make_async_copy(g_hbm, g_ref, in_sem.at[2 * chunks + 1]),
    ]
    for copy in loads + late:
        copy.start()
    barrier = pltpu.get_barrier_semaphore()
    for step in range(1, n_row):
        pl.semaphore_signal(
            barrier, inc=1, device_id=(lax.rem(row + step, n_row), col), device_id_type=MESH
        )
    for step in range(1, n_col):
        pl.semaphore_signal(
            barrier, inc=1, device_id=(row, lax.rem(col + step, n_col)), device_id_type=MESH
        )

    pl.semaphore_wait(barrier, n_row - 1 + n_col - 1)

    def remote(src, dst, send, recv, to):
        return pltpu.make_async_remote_copy(
            src_ref=src, dst_ref=dst, send_sem=send, recv_sem=recv, device_id=to, device_id_type=MESH
        )

    def key_rows(c):
        return (
            remote(kv.at[c, :, nq + halo - halo : nq + halo], kv.at[c, :, 0:halo],
                   kr_s.at[c, 0], kr_r.at[c, 0], (row_down, col)),
            remote(kv.at[c, :, halo : 2 * halo], kv.at[c, :, halo + nq : mid],
                   kr_s.at[c, 1], kr_r.at[c, 1], (row_up, col)),
        )

    def key_cols(c):
        return (
            remote(pack.at[c, :, 0:side], kv.at[c, :, mid : mid + side],
                   kc_s.at[c, 0], kc_r.at[c, 0], (row, col_right)),
            remote(pack.at[c, :, side : 2 * side], kv.at[c, :, mid + side : mid + 2 * side],
                   kc_s.at[c, 1], kc_r.at[c, 1], (row, col_left)),
        )

    def grad_cols(c):
        return (
            remote(strip_out.at[c, :, side : 2 * side], strip_in.at[c, :, side : 2 * side],
                   gc_s.at[c, 0], gc_r.at[c, 0], (row, col_right)),
            remote(strip_out.at[c, :, 0:side], strip_in.at[c, :, 0:side],
                   gc_s.at[c, 1], gc_r.at[c, 1], (row, col_left)),
        )

    def grad_rows(c):
        return (
            remote(rows_out.at[c, :, halo : 2 * halo], rows_in.at[c, :, halo : 2 * halo],
                   gr_s.at[c, 0], gr_r.at[c, 0], (row_down, col)),
            remote(rows_out.at[c, :, 0:halo], rows_in.at[c, :, 0:halo],
                   gr_s.at[c, 1], gr_r.at[c, 1], (row_up, col)),
        )

    def start(copies, after, before):
        pl.when(after)(lambda: copies[0].start())
        pl.when(before)(lambda: copies[1].start())

    def arrive(copies, after, before):
        pl.when(before)(lambda: copies[0].wait_recv())
        pl.when(after)(lambda: copies[1].wait_recv())

    def sent(copies, after, before):
        pl.when(after)(lambda: copies[0].wait_send())
        pl.when(before)(lambda: copies[1].wait_send())

    def send_keys(c):
        loads[2 * c].wait()
        loads[2 * c + 1].wait()
        start(key_rows(c), down, up)

    for c in range(min(2, chunks)):
        send_keys(c)

    @pl.when(jnp.logical_not(up))
    def _():
        kv[:, :, 0:halo, :] = jnp.zeros((chunks, 2, halo, wide), BF16)
        rows_in[:, :, halo : 2 * halo, :] = jnp.zeros((chunks, 2, halo, wide), BF16)

    @pl.when(jnp.logical_not(down))
    def _():
        kv[:, :, halo + nq : mid, :] = jnp.zeros((chunks, 2, halo, wide), BF16)
        rows_in[:, :, 0:halo, :] = jnp.zeros((chunks, 2, halo, wide), BF16)

    @pl.when(jnp.logical_not(left))
    def _():
        kv[:, :, mid : mid + side, :] = jnp.zeros((chunks, 2, side, wide), BF16)
        strip_in[:, :, side : 2 * side, :] = jnp.zeros((chunks, 2, side, wide), BF16)

    @pl.when(jnp.logical_not(right))
    def _():
        kv[:, :, mid + side : mid + 2 * side, :] = jnp.zeros((chunks, 2, side, wide), BF16)
        strip_in[:, :, 0:side, :] = jnp.zeros((chunks, 2, side, wide), BF16)

    tiles_n = table.shape[0]
    cols2 = 2 * tc
    fit = 128 // cols2
    groups = pairs * 2 // fit
    span = 2 * rad + 1
    edge = half - rad
    rel_pad[...] = jnp.zeros_like(rel_pad)

    def fill_rel(a, carry):
        for h in range(pairs * 2):
            at = (h % fit) * cols2
            rel_pad[h // fit, pl.ds(nk - 1 - a, 1), at : at + span] = rel_ref[h, pl.ds(a, 1), :]
        return carry

    lax.fori_loop(0, span, fill_rel, 0)
    steps = tiles_n * 128 // tc
    for g in range(groups):
        x = rel_pad[g]
        for qc in range(tc):
            turned[g, pl.ds(qc, steps, stride=tc), :] = pltpu.roll(x, qc + edge, 1)
        for t in range(tiles_n):
            table[t, g * 128 : (g + 1) * 128, :] = turned[g, t * 128 : (t + 1) * 128, :].T

    sub = lax.broadcasted_iota(jnp.int32, (cols2, nq), 0)
    lane = lax.broadcasted_iota(jnp.int32, (cols2, nq), 1)
    q_row, q_col = lane // tc, lane % tc
    q_high = ext_ref[0, (row * tr) // panel, col]
    q_wide = ext_ref[1, (row * tr) // panel, col]
    q_first = lax.rem(row * tr, panel)
    col_diff = sub - (half - rad) - q_col
    fits = (
        (q_row + q_first < q_high) & (q_col < q_wide) & (col_diff >= 0) & (col_diff <= 2 * rad)
    )
    col_mod = lax.rem(sub + half, tc)
    for kr in range(nk):
        r = row * tr - rad + kr
        inside = (r >= 0) & (r < n_row * tr)
        pr = jnp.clip(r, 0, n_row * tr - 1) // panel
        widths = []
        for shift in (-1, 0, 1):
            pc = jnp.clip(col + shift, 0, panels_c - 1)
            there = inside & (col + shift >= 0) & (col + shift < n_col)
            there = there & (r - pr * panel < ext_ref[0, pr, pc])
            widths.append(jnp.where(there, ext_ref[1, pr, pc], 0))
        width = jnp.where(
            sub < half, widths[0], jnp.where(sub < half + tc, widths[1], widths[2])
        )
        row_diff = kr - q_row
        allowed = fits & (row_diff >= 0) & (row_diff <= 2 * rad) & (col_mod < width)
        mask[kr] = jnp.where(allowed, 0.0, NEG)

    def fill_bias(p, carry):
        for hh in range(2):
            base = pl.multiple_of((p * 2 + hh) * cols2, cols2)
            tiles = [table[t, pl.ds(base, cols2), :] for t in range(tiles_n)]
            lo = hh * 128
            for kr in range(nk):
                off = (nk - 1 - kr) * tc
                t, s = off // 128, off % 128
                x = tiles[t]
                if s:
                    x = pltpu.roll(jnp.where(lane >= s, x, tiles[t + 1]), 128 - s, 1)
                x = x + mask[kr]
                bias[p, mid + kr * half : mid + (kr + 1) * half, lo : lo + 128] = x[:half]
                bias[p, kr * tc : (kr + 1) * tc, lo : lo + 128] = x[half : half + tc]
                at = mid + side + kr * half
                bias[p, at : at + half, lo : lo + 128] = x[half + tc :]
        return carry

    lax.fori_loop(0, pairs, fill_bias, 0)

    q_sub = lax.broadcasted_iota(jnp.int32, (nq, 128), 0)
    ch = lax.broadcasted_iota(jnp.int32, (nq, 128), 1)
    q_valid = (q_sub // tc + q_first < q_high) & (q_sub % tc < q_wide)

    def send_cols(c):
        arrive(key_rows(c), down, up)
        if c + 2 < chunks:
            send_keys(c + 2)
        for i in range(2):
            x = kv[c, i, 0:mid, :].astype(F32).reshape(nk, tc, wide)
            pack[c, i, 0:side, :] = x[:, half:].reshape(side, wide).astype(BF16)
            pack[c, i, side : 2 * side, :] = x[:, :half].reshape(side, wide).astype(BF16)
        start(key_cols(c), right, left)

    def block(x):
        zero = jnp.zeros_like(x)
        return jnp.concatenate(
            [jnp.where(ch < 64, x, zero), jnp.where(ch < 64, zero, x)], axis=0
        ).astype(BF16)

    def compute(c, pp):
        p = c * per + pp
        at = pp * 128
        full = p * 128
        k2 = kv[c, 0, :, pl.ds(at, 128)]
        v2 = kv[c, 1, :, pl.ds(at, 128)]
        qb = block(q_ref[:, pl.ds(full, 128)].astype(F32) * 0.125)
        gb = block(jnp.where(q_valid, g_ref[:, pl.ds(full, 128)].astype(F32), 0.0))
        score = nt(k2, qb) + bias[p]
        weights = jnp.exp(score - jnp.max(score, axis=0, keepdims=True))
        prob = weights * (1.0 / jnp.sum(weights, axis=0, keepdims=True))
        prob_b = prob.astype(BF16)
        dprob = nt(v2, gb)
        delta = jnp.sum(prob_b.astype(F32) * dprob, axis=0, keepdims=True)
        ds = prob * (dprob - delta)
        ds_b = ds.astype(BF16)

        def back(x, scores):
            both = nn(x.T, scores)
            return jnp.concatenate([both[:64, :128], both[64:, 128:]], axis=0).T

        o_ref[:, pl.ds(full, 128)] = jnp.where(q_valid, back(v2, prob_b), 0.0).astype(BF16)
        dq_ref[:, pl.ds(full, 128)] = (back(k2, ds_b) * 0.125).astype(BF16)
        for i, grad in enumerate((nn(ds_b, qb), nn(prob_b, gb))):
            centre[c, i, :, pl.ds(at, 128)] = grad[:mid]
            strip_out[c, i, :, pl.ds(at, 128)] = grad[mid:].astype(BF16)
        for hh in range(2):
            d = ds[:, hh * 128 : (hh + 1) * 128]
            even, odd = jnp.zeros((cols2, nq), F32), jnp.zeros((cols2, nq), F32)
            for turn in range(128 // tc):
                both = [None, None]
                for kr in range(nk):
                    place = nk - 1 - kr
                    if place % (128 // tc) != turn:
                        continue
                    at2 = mid + kr * half
                    x = jnp.concatenate(
                        [d[at2 : at2 + half], d[kr * tc : (kr + 1) * tc],
                         d[side + at2 : side + at2 + half]], axis=0,
                    )
                    i = place // (128 // tc) % 2
                    both[i] = x if both[i] is None else both[i] + x
                shift = turn * tc
                if shift:
                    one, two = (pltpu.roll(x, shift, 1) for x in both)
                    even = even + jnp.where(lane >= shift, one, two)
                    odd = odd + jnp.where(lane >= shift, two, one)
                else:
                    even, odd = even + both[0], odd + both[1]
            base = (p * 2 + hh) * cols2
            dtable[0, base : base + cols2, :] = even
            dtable[1, base : base + cols2, :] = odd

    def send_rows(c):
        arrive(grad_cols(c), right, left)
        for i in range(2):
            x = centre[c, i].reshape(nk, tc, wide)
            y = jnp.concatenate(
                [strip_in[c, i, side : 2 * side, :].astype(F32).reshape(nk, half, wide),
                 strip_in[c, i, 0:side, :].astype(F32).reshape(nk, half, wide)], axis=1,
            )
            total = (x + y).reshape(mid, wide)
            rows_out[c, i, 0:halo, :] = total[:halo].astype(BF16)
            rows_out[c, i, halo : 2 * halo, :] = total[halo + nq :].astype(BF16)
            centre[c, i, halo : halo + nq, :] = total[halo : halo + nq]
        start(grad_rows(c), down, up)

    for copy in late:
        copy.wait()
    def spread(g, slots, me, count, send, recv, to):
        return [
            remote(part.at[g], slots.at[g, me], send.at[g, k], recv.at[g, k],
                   to(lax.rem(me + k, count)))
            for k in range(1, count)
        ]

    def over_rows(g):
        return spread(g, slots_r, row, n_row, br_s, br_r, lambda k: (k, col))

    def over_cols(g):
        return spread(g, slots_c, col, n_col, bc_s, bc_r, lambda k: (row, k))

    def gather_bias(g):
        for t in range(2):
            turned[g, t * 128 : (t + 1) * 128, :] = dtable[t, g * 128 : (g + 1) * 128, :].T
        total = jnp.zeros((16, 128), F32)
        for qc in range(tc):
            x = turned[g, pl.ds(qc, 16, stride=tc), :]
            total = total + pltpu.roll(x, 128 - qc - edge, 1)
        part[g] = total
        for copy in over_rows(g):
            copy.start()
        slots_r[g, row] = total

    def turn_bias(g):
        for copy in over_rows(g):
            copy.wait()
        total = slots_r[g, 0]
        for k in range(1, n_row):
            total = total + slots_r[g, k]
        part[g] = total
        for copy in over_cols(g):
            copy.start()
        slots_c[g, col] = total

    group_pairs = fit // 2
    send_cols(0)
    for c in range(chunks):
        if c + 1 < chunks:
            send_cols(c + 1)
        arrive(key_cols(c), right, left)
        for pp in range(per):
            compute(c, pp)
        start(grad_cols(c), right, left)
        if c:
            send_rows(c - 1)
        done = (c + 1) * per
        if done % group_pairs == 0:
            gather_bias(done // group_pairs - 1)
        elif done // group_pairs:
            turn_bias(done // group_pairs - 1)
    send_rows(chunks - 1)
    turn_bias(groups - 1)

    for c in range(chunks):
        arrive(grad_rows(c), down, up)
        for i, out in enumerate((dk_ref, dv_ref)):
            x = centre[c, i, halo : halo + nq, :]
            fill = jnp.zeros((nq - halo, wide), F32)
            x = x + jnp.concatenate([rows_in[c, i, halo : 2 * halo, :].astype(F32), fill], axis=0)
            x = x + jnp.concatenate([fill, rows_in[c, i, 0:halo, :].astype(F32)], axis=0)
            out[:, c * wide : (c + 1) * wide] = x.astype(BF16)
    for g in range(groups):
        for copy in over_cols(g):
            copy.wait()
        total = slots_c[g, 0]
        for k in range(1, n_col):
            total = total + slots_c[g, k]
        part[g] = total

    def give_rel(a, carry):
        for h in range(pairs * 2):
            at = (h % fit) * cols2
            row_at = lax.rem(nk - 1 - a, 16)
            rb_ref[h, pl.ds(a, 1), :] = part[h // fit, pl.ds(row_at, 1), at : at + span]
        return carry

    lax.fori_loop(0, span, give_rel, 0)
    for c in range(chunks):
        sent(key_rows(c), down, up)
        sent(key_cols(c), right, left)
        sent(grad_cols(c), right, left)
        sent(grad_rows(c), down, up)


def hand_over(*refs):
    sources, targets, (held, sems) = refs[:4], refs[4:8], refs[8:]
    first = [pltpu.make_async_copy(sources[i], held.at[i], sems.at[0, i]) for i in range(4)]
    second = [pltpu.make_async_copy(held.at[i], targets[i], sems.at[1, i]) for i in range(4)]
    for copy in first:
        copy.start()
    for before, after in zip(first, second):
        before.wait()
        after.start()
    for copy in second:
        copy.wait()


def shards(n_row, n_col, queries, keys, values, d_out, extents, rel_bias):
    tr, tc, channels = queries.shape
    heads, span = rel_bias.shape[0], rel_bias.shape[1]
    rad = (span - 1) // 2
    nq, nk = tr * tc, tr + 2 * rad
    wide = channels // CHUNKS
    mid, side, halo = nk * tc, nk * (tc // 2), rad * tc
    groups = heads * 2 * tc // 128
    lanes = -(-((nk + tr - 1) * tc) // 128) * 128
    flat = [x.reshape(nq, channels) for x in (queries, keys, values, d_out)]
    vmem = pl.BlockSpec(memory_space=pltpu.VMEM)
    hbm = pl.BlockSpec(memory_space=pltpu.HBM)
    dma = pltpu.SemaphoreType.DMA
    out = jax.ShapeDtypeStruct((nq, channels), BF16)
    *big, d_rel = pl.pallas_call(
        functools.partial(kernel, n_row, n_col, tr, tc, rad),
        out_shape=[out, out, out, out, jax.ShapeDtypeStruct(rel_bias.shape, F32)],
        in_specs=[hbm] * 4 + [pl.BlockSpec(memory_space=pltpu.SMEM), vmem],
        out_specs=[vmem] * 5,
        scratch_shapes=[
            pltpu.VMEM((nq, channels), BF16),
            pltpu.VMEM((nq, channels), BF16),
            pltpu.VMEM((CHUNKS, 2, mid + 2 * side, wide), BF16),
            pltpu.VMEM((CHUNKS, 2, 2 * side, wide), BF16),
            pltpu.VMEM((channels // 128, mid + 2 * side, 256), F32),
            pltpu.VMEM((nk, 2 * tc, nq), F32),
            pltpu.VMEM((groups, lanes // tc, 128), F32),
            pltpu.VMEM((groups, lanes, 128), F32),
            pltpu.VMEM((lanes // 128, heads * 2 * tc, 128), F32),
            pltpu.VMEM((2, heads * 2 * tc, 128), F32),
            pltpu.VMEM((CHUNKS, 2, mid, wide), F32),
            pltpu.VMEM((CHUNKS, 2, 2 * side, wide), BF16),
            pltpu.VMEM((CHUNKS, 2, 2 * side, wide), BF16),
            pltpu.VMEM((CHUNKS, 2, 2 * halo, wide), BF16),
            pltpu.VMEM((CHUNKS, 2, 2 * halo, wide), BF16),
            pltpu.VMEM((groups, 16, 128), F32),
            pltpu.VMEM((groups, n_row, 16, 128), F32),
            pltpu.VMEM((groups, n_col, 16, 128), F32),
        ]
        + [dma((2 * CHUNKS + 2,))]
        + [dma((CHUNKS, 2))] * 8
        + [dma((groups, n_row))] * 2
        + [dma((groups, n_col))] * 2,
        compiler_params=pltpu.CompilerParams(
            collective_id=0, has_side_effects=True, vmem_limit_bytes=63 * 1024 * 1024
        ),
        cost_estimate=pl.CostEstimate(
            flops=12 * 12 * 128 * 640 * 64, bytes_accessed=8 * 200000, transcendentals=12 * 128 * 640
        ),
    )(*flat, extents, rel_bias)
    big = pl.pallas_call(
        hand_over,
        out_shape=[out] * 4,
        in_specs=[hbm] * 4,
        out_specs=[hbm] * 4,
        scratch_shapes=[pltpu.VMEM((4, nq, channels), BF16), dma((2, 4))],
        compiler_params=pltpu.CompilerParams(vmem_limit_bytes=63 * 1024 * 1024),
    )(*big)
    return (*(x.reshape(tr, tc, channels) for x in big), d_rel)


def solution(mesh):
    tile = P("row", "col", None)
    return jax.shard_map(
        functools.partial(shards, mesh.shape["row"], mesh.shape["col"]),
        mesh=mesh,
        in_specs=(tile, tile, tile, tile, P(), P()),
        out_specs=(tile, tile, tile, tile, P()),
        check_vma=False,
    )
```
